128 devices in a mesh: seq: 8 (over y, core), tensor: 16 (over z, x).
Axes of the slice: x: 4, y: 4, z: 4, core: 2. Of those that a mesh axis runs over, the one named last changes fastest.
Arguments:
- hidden_rows: bfloat16 [24576, 2560], P(('seq', 'tensor')), may hold values from -6 to 6
- value_weight: bfloat16 [2560, 5120], P(None, 'tensor'), may hold values from -0.125 to 0.125
- gating_weight: bfloat16 [2560, 5120], P(None, 'tensor'), may hold values from -0.125 to 0.125
- state_weight: bfloat16 [2560, 256], replicated, may hold values from -0.125 to 0.125
- step_weight: bfloat16 [2560, 80], P(None, 'tensor'), may hold values from -0.125 to 0.125
- value_kernel: float32 [4, 5120], P(None, 'tensor'), may hold values from -3 to 3
- state_kernel: float32 [4, 256], replicated, may hold values from -3 to 3
- step_bias: float32 [80], P('tensor'), may hold values from -4.5 to -3.5
- decay_log: float32 [80], P('tensor'), may hold values from -10 to 1.5
- skip_scale: float32 [80], P('tensor'), may hold values from 0.1 to 4
- norm_scale: float32 [5120], P('tensor'), may hold values from 0.5 to 1.5
- document_lengths: int32 [16], replicated, may hold values from 1 to 12288, 24576 in all
Outputs:
- layer_out: bfloat16 [24576, 5120], P('seq', 'tensor')
The draws below stay inside these ranges and needn't reach their ends.
Inputs may be any that keep to these rules, and one draw needn't show every extreme that they name: `document_lengths`: the 16 documents of the pack in order; their lengths sum to 24576.
All inputs are finite; a program needn't handle non-finite values.
Results may differ from the reference program's by a relative error of at most 0.0061.
Values may be sent and summed in bfloat16 or wider, within the bound.
No kernel may reach another device: no remote copies, remote signals or barrier semaphores. Data moves between devices by JAX's collectives and lax.ppermute only.
A program may use at most 128 MiB of HBM per device.

```python
import math
import jax
import jax.numpy as jnp
import numpy as np
from jax import lax

D = 2560
H = 80
P_SIZE = 64
N = 128
KCONV = 4
Q = 256
DOCS = 16
SEQ = 24576


def draw_decay_log(key, part):
    key = jax.random.fold_in(key, 5)
    pick_key, slow_key, fast_key = jax.random.split(key, 3)
    slow_share = 0.5
    slow_heads = jax.random.uniform(pick_key, (H,)) < slow_share
    slow_rate = jnp.exp(jax.random.uniform(slow_key, (H,), minval=jnp.log(0.3 / SEQ), maxval=jnp.log(2.0 / SEQ)))
    fast_rate = jnp.exp(jax.random.uniform(fast_key, (H,), minval=jnp.log(1.0 / 50.0), maxval=jnp.log(1.0 / 8.0)))
    rate = jnp.where(slow_heads, slow_rate, fast_rate)
    return jnp.log(rate / 0.03).astype(jnp.float32)


def draw_skip_scale(key, part):
    key = jax.random.fold_in(key, 9)
    ramp = jnp.arange(H, dtype=jnp.float32) / (H - 1)
    base_value = jax.random.uniform(key, (H,), minval=0.5, maxval=1.5)
    slope = 0.4 + 1.2 * ramp
    return (base_value * slope).astype(jnp.float32)


def block_levels(rng, shape, pieces, low, top_value):
    def one(position, shards_of):
        draws = jax.random.uniform(jax.random.fold_in(jax.random.fold_in(rng, 6), position), (shards_of,), jnp.float32, low / len(pieces), top_value / len(pieces))
        return jnp.repeat(jnp.exp(draws), shape[position] // shards_of).reshape((-1,) + (1,) * (len(shape) - position - 1))

    gain = one(*pieces[0])
    for cut in pieces[1:]:
        gain = gain * one(*cut)
    return gain


def profile(number_of, total, limit, skew):
    portions = [(1 << 20) // math.isqrt(standing ** skew) + 1 for standing in range(2, number_of + 1)]
    rest, given = total - limit - (number_of - 1), [1] * (number_of - 1)
    while rest > 0:
        movable = [i for i in range(number_of - 1) if given[i] < limit]
        pool, budget = sum([portions[i] for i in movable]), rest
        for i in movable:
            addition = min(limit - given[i], max(1, budget * portions[i] // pool), rest)
            given[i] = given[i] + addition
            rest = rest - addition
    return np.array([limit] + given)


def uneven_parts(key, amount, total, reach, skew):
    if amount == 2:
        one = jax.random.randint(key, (), max(1, total - reach), min(reach, total - 1) + 1)
        return jnp.stack([one, total - one])
    tallies = jnp.asarray(profile(amount, total, reach, skew), jnp.int32)
    couples = (amount - 1) // 2
    source_of, receiver = tallies[1:1 + 2 * couples:2], tallies[2:2 + 2 * couples:2]
    slack = jnp.minimum(source_of - 1, reach - receiver)
    passed = jax.random.randint(jax.random.fold_in(key, 1), (couples,), 0, 1 << 20) % (slack + 1)
    tallies = tallies.at[1:1 + 2 * couples:2].set(source_of - passed).at[2:2 + 2 * couples:2].set(receiver + passed)
    return tallies[jax.random.permutation(jax.random.fold_in(key, 2), amount)]


def bell_draw(own_key, shape, scale, bound, cuts=(), kind=jnp.bfloat16):
    entries = scale * jax.random.normal(own_key, shape, jnp.float32)
    if cuts:
        entries = entries * block_levels(own_key, shape, cuts, -0.22, 0.18)
    return jnp.clip(entries, -bound, bound).astype(kind)


def setup_inputs(seed: int = 0) -> dict:
    splits = jax.random.split(jax.random.key(seed), 13)
    return {
        "hidden_rows": bell_draw(splits[0], (SEQ, D), 1.0, 6.0, ((0, 128),)),
        "value_weight": bell_draw(splits[1], (D, H * P_SIZE), D ** -0.5, 0.125, ((1, 16),)),
        "gating_weight": bell_draw(splits[2], (D, H * P_SIZE), D ** -0.5, 0.125, ((1, 16),)),
        "state_weight": bell_draw(splits[3], (D, 2 * N), D ** -0.5, 0.125),
        "step_weight": bell_draw(splits[4], (D, H), D ** -0.5, 0.125, ((1, 16),)),
        "value_kernel": bell_draw(splits[5], (KCONV, H * P_SIZE), KCONV ** -0.5, 3.0, ((1, 16),), jnp.float32),
        "state_kernel": bell_draw(splits[6], (KCONV, 2 * N), KCONV ** -0.5, 3.0, (), jnp.float32),
        "step_bias": jnp.clip(-4.5 + 1.0 * jax.random.uniform(splits[7], (H,), jnp.float32) ** block_levels(splits[7], (H,), ((0, 16),), -0.2, 0.2), -4.5, -3.5),
        "decay_log": draw_decay_log(jax.random.fold_in(splits[12], 71), 0),
        "skip_scale": draw_skip_scale(jax.random.fold_in(splits[12], 71), 0),
        "norm_scale": jnp.clip(1.0 + 0.1 * jax.random.normal(splits[10], (H * P_SIZE,), jnp.float32), 0.5, 1.5),
        "document_lengths": uneven_parts(splits[11], DOCS, SEQ, SEQ // 2, 2).astype(jnp.int32),
    }


def document_ids(positions, document_lengths):
    boundary = jnp.cumsum(document_lengths) - document_lengths
    hits = (positions[:, None] >= boundary[None, :]).astype(jnp.int32)
    return (lax.optimization_barrier(jnp.sum(hits, axis=1)) - 1).astype(jnp.int32)

def convolve(raw_inputs, kernel, documents_ext, taps):
    length = raw_inputs.shape[0]
    padded = jnp.concatenate([jnp.zeros((taps - 1, raw_inputs.shape[1]), raw_inputs.dtype), raw_inputs], 0)
    current = documents_ext[taps - 1:]
    row_total = jnp.zeros(raw_inputs.shape, jnp.float32)
    for offset in range(taps):
        first_row = taps - 1 - offset
        shifted = padded[first_row:first_row + length].astype(jnp.float32)
        keep_mask = (documents_ext[first_row:first_row + length] == current).astype(jnp.float32)
        row_total = row_total + kernel[offset][None, :] * shifted * keep_mask[:, None]
    return jax.nn.silu(row_total).astype(jnp.bfloat16)

def block_update(carry_state, inputs, skip_scale):
    values, input_map, output_map, step_size, log_decay, documents, before = inputs
    precise = lax.Precision.HIGHEST
    running = jnp.cumsum(log_decay, axis=0)
    index_range = jnp.arange(documents.shape[0])
    allowed = (documents[:, None] == documents[None, :]) & (index_range[:, None] >= index_range[None, :])
    spread = running[:, None, :] - running[None, :, :]
    factor = jnp.where(allowed[:, :, None], jnp.exp(jnp.where(allowed[:, :, None], spread, 0.0)), 0.0)
    scores = jnp.dot(output_map, input_map.T, precision=precise)
    mixing = scores[:, :, None] * factor * step_size[None, :, :]
    inner_part = jnp.einsum('ijh,jhp->ihp', mixing, values, precision=precise)
    carried = (documents == before).astype(jnp.float32)
    entering = jnp.einsum('in,hnp->ihp', output_map, carry_state, precision=precise)
    entering = entering * (carried[:, None] * jnp.exp(running))[:, :, None]
    tail_weight = jnp.where((documents == documents[-1])[:, None], jnp.exp(running[-1][None, :] - running), 0.0) * step_size
    update = jnp.einsum('jn,jhp->hnp', input_map, values * tail_weight[:, :, None], precision=precise)
    passing = carried[-1] * jnp.exp(running[-1])
    new_state = passing[:, None, None] * carry_state + update
    output = inner_part + entering + skip_scale[None, :, None] * values
    return (new_state, output)

def reference(hidden_rows, value_weight, gating_weight, state_weight, step_weight, value_kernel, state_kernel, step_bias, decay_log, skip_scale, norm_scale, document_lengths):
    length = hidden_rows.shape[0]
    inner_width = value_weight.shape[1]
    head_count = step_weight.shape[1]
    head_width = inner_width // head_count
    state_count = state_weight.shape[1] // 2
    joined = jnp.concatenate([value_weight, gating_weight, state_weight, step_weight], 1)
    projected = jnp.dot(hidden_rows, joined, preferred_element_type=jnp.float32).astype(jnp.bfloat16)
    value_raw = projected[:, :inner_width]
    gating_raw = projected[:, inner_width:2 * inner_width]
    map_raw = projected[:, 2 * inner_width:2 * inner_width + 2 * state_count]
    step_raw = projected[:, 2 * inner_width + 2 * state_count:]
    positions = jnp.arange(-(KCONV - 1), length, dtype=jnp.int32)
    documents_ext = document_ids(positions, document_lengths)
    documents = documents_ext[KCONV - 1:]
    before_all = documents_ext[KCONV - 2:KCONV - 2 + length]
    raw_inputs = jnp.concatenate([value_raw, map_raw], 1)
    kernel = jnp.concatenate([value_kernel, state_kernel], 1)
    conv_out = convolve(raw_inputs, kernel, documents_ext, KCONV)
    values = conv_out[:, :inner_width].astype(jnp.float32).reshape(length, head_count, head_width)
    input_map = conv_out[:, inner_width:inner_width + state_count].astype(jnp.float32)
    output_map = conv_out[:, inner_width + state_count:].astype(jnp.float32)
    step_size = jax.nn.softplus(step_raw.astype(jnp.float32) + step_bias[None, :])
    log_decay = -jnp.exp(decay_log)[None, :] * step_size
    block_count = length // Q
    inputs = (values.reshape(block_count, Q, head_count, head_width), input_map.reshape(block_count, Q, state_count), output_map.reshape(block_count, Q, state_count), step_size.reshape(block_count, Q, head_count), log_decay.reshape(block_count, Q, head_count), documents.reshape(block_count, Q), before_all.reshape(block_count, Q)[:, 0])

    def advance(carry_state, block_inputs):
        return block_update(carry_state, block_inputs, skip_scale)
    start_state = jnp.zeros((head_count, state_count, head_width), jnp.float32)
    unused, outputs = lax.scan(advance, start_state, inputs)
    ssd_out = outputs.reshape(length, inner_width)
    gated_out = ssd_out * jax.nn.silu(gating_raw.astype(jnp.float32))
    mean_square = lax.optimization_barrier(jnp.mean(gated_out * gated_out, axis=1, keepdims=True))
    return (gated_out * lax.rsqrt(mean_square + 1e-05) * norm_scale[None, :]).astype(jnp.bfloat16)
```

```python
import functools

import jax
import jax.numpy as jnp
from jax import lax
from jax.experimental import pallas as pl
from jax.experimental.pallas import tpu as pltpu
from jax.sharding import PartitionSpec as P

KCONV = 4
Q = 256
LANES = 128
SIDE = 4
REACH = 4
F32 = jnp.float32
BF16 = jnp.bfloat16


def dot(a, b, contract=((1,), (0,))):
    return lax.dot_general(a, b, (contract, ((), ())), preferred_element_type=F32)


def halves(a):
    high = a.astype(BF16)
    return high, (a - high.astype(F32)).astype(BF16)


def thirds(a):
    high = a.astype(BF16)
    rest = a - high.astype(F32)
    middle = rest.astype(BF16)
    return high, middle, (rest - middle.astype(F32)).astype(BF16)


def spread_heads(a, expand):
    high, low = halves(a)
    return dot(high, expand) + dot(low, expand)


def silu(v):
    half = 0.5 * v
    return half + half * jnp.tanh(half)


def ssd_kernel(
    heads,
    lane0,
    step_col,
    wide,
    proj_ref,
    rim_ref,
    seg_ref,
    taps_ref,
    vectors_ref,
    skip_ref,
    expand_ref,
    y_ref,
    reach_ref,
    map_ref,
    state_ref,
    rows,
    state,
    total,
):
    block = pl.program_id(0)
    raw_wide = wide + 2 * LANES

    @pl.when(block == 0)
    def _():
        rows[0:8, :] = rim_ref[...].astype(F32)
        state[...] = jnp.zeros_like(state)
        total[...] = jnp.zeros_like(total)

    rows[8:, :wide] = proj_ref[:, :wide].astype(F32)
    rows[8:, wide:] = proj_ref[:, 2 * wide : 2 * wide + 2 * LANES].astype(F32)
    first = block * Q
    seg = seg_ref[...] - first
    place = lax.broadcasted_iota(jnp.int32, (Q, LANES), 0)
    keep = [place - k >= seg for k in range(1, KCONV)]
    pieces = []
    for tile in range(raw_wide // LANES):
        at = slice(tile * LANES, (tile + 1) * LANES)
        sums = taps_ref[0:1, at] * rows[8:, at]
        for k in range(1, KCONV):
            sums = sums + jnp.where(keep[k - 1], taps_ref[k : k + 1, at] * rows[8 - k : 8 - k + Q, at], 0.0)
        pieces.append(silu(sums).astype(BF16))
    rows[0:8, :] = rows[Q : Q + 8, :]
    tiles = wide // LANES
    values = jnp.concatenate([p.astype(F32) for p in pieces[:tiles]], 1)
    input_map, output_map = pieces[tiles], pieces[tiles + 1]
    map_ref[...] = output_map

    v = proj_ref[:, step_col : step_col + LANES].astype(F32) + vectors_ref[0:1, :]
    step = jnp.maximum(v, 0.0) + jnp.log(1.0 + jnp.exp(-jnp.abs(v)))
    decay = vectors_ref[1:2, :] * step
    ii = lax.broadcasted_iota(jnp.int32, (Q, Q), 0)
    jj = lax.broadcasted_iota(jnp.int32, (Q, Q), 1)
    causal = (jj <= ii).astype(F32).astype(BF16)
    running = sum(dot(causal, part) for part in thirds(decay))
    running_t = running.T
    barred = jnp.where((jj <= ii) & (jj >= jnp.concatenate([seg, seg], 1)), 0.0, -1e30)
    last = running[Q - 1 : Q, :]
    last_seg = seg[Q - 1 : Q, :]
    carried = jnp.where(seg < 0, jnp.exp(running), 0.0)
    tail = jnp.where(place >= last_seg, jnp.exp(last - running), 0.0) * step
    reach_ref[...] = jnp.where(seg + first < 0, jnp.exp(total[0:1, :] + running), 0.0)
    total[0:1, :] = total[0:1, :] + last

    expand = expand_ref[...]
    carried_wide = spread_heads(carried, expand)
    stepped = values * spread_heads(step, expand)
    tailed = (values * spread_heads(tail, expand)).astype(BF16)
    scores = dot(output_map, input_map, ((1,), (1,)))
    left = lax.broadcasted_iota(jnp.int32, (Q, LANES), 1) < LANES // 2
    outs = []
    for tile in range(tiles):
        pair = stepped[:, tile * LANES : (tile + 1) * LANES]
        acc = None
        for side in range(2):
            head = 2 * tile + side
            if head >= heads:
                continue
            lane = lane0 + head
            factor = jnp.exp(running[:, lane : lane + 1] - running_t[lane : lane + 1, :] + barred)
            mixing = (scores * factor).astype(BF16)
            mine = jnp.where(left if side == 0 else ~left, pair, 0.0).astype(BF16)
            term = dot(mixing, mine)
            acc = term if acc is None else acc + term
        outs.append(acc)
    inner = jnp.concatenate(outs, 1)
    entering = dot(output_map, state[...].astype(BF16)) * carried_wide
    y_ref[...] = inner + entering + skip_ref[0:1, :] * values
    state[...] = carried_wide[Q - 1 : Q, :] * state[...] + dot(input_map, tailed, ((0,), (0,)))

    @pl.when(block == pl.num_programs(0) - 1)
    def _():
        state_ref[0:LANES, :] = state[...]
        whole = jnp.where(last_seg + first < 0, jnp.exp(total[0:1, :]), 0.0)
        state_ref[LANES:, :] = spread_heads(jnp.broadcast_to(whole, (8, LANES)), expand)


def ssd_pass(proj, rim, seg, taps, vectors, skip, expand, heads, lane0, step_col, wide):
    count = proj.shape[0]
    width = proj.shape[1]
    raw_wide = wide + 2 * LANES
    by_block = lambda w: pl.BlockSpec((Q, w), lambda i: (i, 0))
    whole = lambda a: pl.BlockSpec(a.shape, lambda i: (0,) * a.ndim)
    return pl.pallas_call(
        functools.partial(ssd_kernel, heads, lane0, step_col, wide),
        grid=(count // Q,),
        in_specs=[by_block(width), whole(rim), by_block(LANES), whole(taps), whole(vectors), whole(skip), whole(expand)],
        out_specs=[by_block(wide), by_block(LANES), by_block(LANES), pl.BlockSpec((LANES + 8, wide), lambda i: (0, 0))],
        out_shape=[
            jax.ShapeDtypeStruct((count, wide), F32),
            jax.ShapeDtypeStruct((count, LANES), F32),
            jax.ShapeDtypeStruct((count, LANES), BF16),
            jax.ShapeDtypeStruct((LANES + 8, wide), F32),
        ],
        scratch_shapes=[
            pltpu.VMEM((Q + 8, raw_wide), F32),
            pltpu.VMEM((LANES, wide), F32),
            pltpu.VMEM((8, LANES), F32),
        ],
        compiler_params=pltpu.CompilerParams(vmem_limit_bytes=48 * 1024 * 1024),
        name="ssd_pass",
    )(proj, rim, seg, taps, vectors, skip, expand)


def gate_kernel(*refs):
    parts = refs[:REACH]
    y_ref, reach_ref, map_ref, gate_ref, expand_ref, gated_ref, squares_ref, entering = refs[REACH:]

    @pl.when(pl.program_id(0) == 0)
    def _():
        sofar = parts[-1][0:LANES, :]
        for part in parts[-2::-1]:
            sofar = part[0:LANES, :] + part[LANES : LANES + 1, :] * sofar
        entering[...] = sofar.astype(BF16)

    y = y_ref[...] + dot(map_ref[...], entering[...]) * spread_heads(reach_ref[...], expand_ref[...])
    gated = y * silu(gate_ref[...].astype(F32))
    gated_ref[...] = gated
    ones = jnp.ones((8, gated.shape[1]), BF16)
    squares_ref[0] = sum(dot(ones, part, ((1,), (1,))) for part in halves(gated * gated))


def gate_pass(parts, y, reach, out_map, proj, expand):
    count, wide = y.shape
    by_block = lambda w, c=0: pl.BlockSpec((Q, w), lambda i: (i, c))
    whole = lambda a: pl.BlockSpec(a.shape, lambda i: (0,) * a.ndim)
    return pl.pallas_call(
        gate_kernel,
        grid=(count // Q,),
        in_specs=[whole(p) for p in parts] + [by_block(wide), by_block(LANES), by_block(LANES), by_block(wide, 1), whole(expand)],
        out_specs=[by_block(wide), pl.BlockSpec((1, 8, Q), lambda i: (i, 0, 0))],
        out_shape=[
            jax.ShapeDtypeStruct((count, wide), F32),
            jax.ShapeDtypeStruct((count // Q, 8, Q), F32),
        ],
        scratch_shapes=[pltpu.VMEM((LANES, wide), BF16)],
        compiler_params=pltpu.CompilerParams(vmem_limit_bytes=48 * 1024 * 1024),
        name="gate_pass",
    )(*parts, y, reach, out_map, proj, expand)


def norm_kernel(channels, parts, *refs):
    squares = refs[:parts]
    gated_ref, gain_ref, out_ref = refs[parts:]
    total = squares[0][0]
    for part in squares[1:]:
        total = total + part[0]
    scale = lax.rsqrt(total / channels + 1e-5)
    ones = jnp.ones((8, LANES), BF16)
    first = lax.broadcasted_iota(jnp.int32, (8, Q), 0) == 0
    scale = jnp.where(first, scale, 0.0)
    column = sum(dot(part, ones, ((0,), (0,))) for part in thirds(scale))
    width = out_ref.shape[1]
    for tile in range(0, width, LANES):
        w = min(LANES, width - tile)
        out_ref[:, tile : tile + w] = (
            gated_ref[:, tile : tile + w] * column[:, :w] * gain_ref[0:1, tile : tile + w]
        ).astype(BF16)


def norm_pass(squares, gated, gain, channels, width):
    count, wide = gated.shape
    whole = lambda a: pl.BlockSpec(a.shape, lambda i: (0,) * a.ndim)
    return pl.pallas_call(
        functools.partial(norm_kernel, channels, len(squares)),
        grid=(count // Q,),
        in_specs=[pl.BlockSpec((1, 8, Q), lambda i: (i, 0, 0)) for _ in squares]
        + [pl.BlockSpec((Q, wide), lambda i: (i, 0)), whole(gain)],
        out_specs=pl.BlockSpec((Q, width), lambda i: (i, 0)),
        out_shape=jax.ShapeDtypeStruct((count, width), BF16),
        compiler_params=pltpu.CompilerParams(vmem_limit_bytes=48 * 1024 * 1024),
        name="norm_pass",
    )(*squares, gated, gain)


def along_x(by):
    return [(z * SIDE + x, z * SIDE + (x + by) % SIDE) for z in range(SIDE) for x in range(SIDE)]


def along_z(by):
    return [(z * SIDE + x, (z + by) % SIDE * SIDE + x) for z in range(SIDE) for x in range(SIDE)]


def from_behind(array, by):
    length = lax.axis_size("seq")
    return lax.ppermute(array, "seq", [(i, i + by) for i in range(length - by)])


def padded(a, width):
    return jnp.pad(a, [(0, 0)] * (a.ndim - 1) + [(0, width - a.shape[-1])])


def on_device(
    hidden_rows,
    value_weight,
    gating_weight,
    state_weight,
    step_weight,
    value_kernel,
    state_kernel,
    step_bias,
    decay_log,
    skip_scale,
    norm_scale,
    document_lengths,
):
    members = lax.axis_size("tensor")
    count = hidden_rows.shape[0] * members
    inner = value_weight.shape[1]
    heads = step_weight.shape[1]
    head_width = inner // heads
    wide = -(-inner // LANES) * LANES
    lane0 = inner % LANES
    step_col = inner - lane0
    raw_wide = wide + 2 * LANES
    joined = jnp.concatenate(
        [
            padded(jnp.concatenate([value_weight, step_weight], 1), wide),
            padded(gating_weight, wide),
            state_weight,
        ],
        1,
    )
    taps = jnp.concatenate([padded(value_kernel, wide), state_kernel], 1)
    taps = jnp.pad(taps, ((0, 8 - KCONV), (0, 0)))
    at_lanes = lambda a: jnp.pad(a, (lane0, LANES - lane0 - heads))
    vectors = jnp.pad(jnp.stack([at_lanes(step_bias), at_lanes(-jnp.exp(decay_log))]), ((0, 6), (0, 0)))
    wide_rows = lambda a: jnp.broadcast_to(padded(a, wide), (8, wide))
    skip = wide_rows(jnp.repeat(skip_scale, head_width))
    gain = wide_rows(norm_scale)
    expand = (
        jnp.arange(LANES)[:, None] - lane0 == (jnp.arange(wide) // head_width)[None, :]
    ).astype(BF16)
    starts = jnp.cumsum(document_lengths) - document_lengths
    row_offset = lax.axis_index("seq") * count
    positions = row_offset + jnp.arange(count, dtype=jnp.int32)
    seg = jnp.max(jnp.where(positions[:, None] >= starts[None, :], starts[None, :], 0), axis=1) - row_offset
    seg = jnp.broadcast_to(seg[:, None], (count, LANES)).astype(jnp.int32)

    gathered = lax.all_gather(hidden_rows, "tensor", axis=0, tiled=True)
    project = lambda rows: jnp.dot(rows, joined, preferred_element_type=F32).astype(BF16)
    proj = project(gathered)
    ends = proj[count - 8 :]
    rim = from_behind(jnp.concatenate([ends[:, :wide], ends[:, 2 * wide :]], 1), 1)
    y, reach, out_map, summary = ssd_pass(
        proj, rim, seg, taps, vectors, skip, expand, heads, lane0, step_col, wide
    )
    parts = [from_behind(summary, by) for by in range(1, REACH + 1)]
    gated, squares = gate_pass(parts, y, reach, out_map, proj, expand)
    row_sum = squares + sum(lax.ppermute(squares, "tensor", along_x(by)) for by in range(1, SIDE))
    shares = [row_sum] + [lax.ppermute(row_sum, "tensor", along_z(by)) for by in range(1, SIDE)]
    return norm_pass(shares, gated, gain, inner * members, inner)


def solution(mesh):
    in_specs = (
        P(("seq", "tensor"), None),
        P(None, "tensor"),
        P(None, "tensor"),
        P(),
        P(None, "tensor"),
        P(None, "tensor"),
        P(),
        P("tensor"),
        P("tensor"),
        P("tensor"),
        P("tensor"),
        P(),
    )
    out_specs = P("seq", "tensor")
    return jax.shard_map(
        on_device, mesh=mesh, in_specs=in_specs, out_specs=out_specs, check_vma=False
    )
```

```python
import functools

import jax
import jax.numpy as jnp
from jax import lax
from jax.experimental import pallas as pl
from jax.experimental.pallas import tpu as pltpu
from jax.sharding import PartitionSpec as P

KCONV = 4
Q = 256
LANES = 128
SIDE = 4
REACH = 4
F32 = jnp.float32
BF16 = jnp.bfloat16


def dot(a, b, contract=((1,), (0,))):
    return lax.dot_general(a, b, (contract, ((), ())), preferred_element_type=F32)


def thirds(a):
    high = a.astype(BF16)
    rest = a - high.astype(F32)
    middle = rest.astype(BF16)
    return high, middle, (rest - middle.astype(F32)).astype(BF16)


def silu(v):
    half = 0.5 * v
    return half + half * jnp.tanh(half)


def ssd_kernel(
    heads,
    value_ref,
    in_ref,
    out_ref,
    step_ref,
    rim_ref,
    seg_ref,
    taps_ref,
    vectors_ref,
    skip_ref,
    y_ref,
    reach_ref,
    map_ref,
    state_ref,
    before,
    state,
    total,
):
    block = pl.program_id(0)
    inner = value_ref.shape[0]
    head_width = inner // heads

    @pl.when(block == 0)
    def _():
        before[...] = rim_ref[...].astype(F32)
        state[...] = jnp.zeros_like(state)
        total[...] = jnp.zeros_like(total)

    first = block * Q
    seg = seg_ref[...] - first
    place = lax.broadcasted_iota(jnp.int32, (1, Q), 1)
    keep = [jnp.broadcast_to(jnp.where(place - k >= seg, 1.0, 0.0), (8, Q)) for k in range(1, KCONV)]

    def convolved(ref, at, base):
        raw = ref[at : at + 8, :]
        rows = slice(base + at, base + at + 8)
        ext = jnp.concatenate([before[rows, :], raw], 1)
        taps = [jnp.concatenate([taps_ref[k, rows, :]] * (Q // LANES), 1) for k in range(KCONV)]
        sums = taps[0] * raw
        for k in range(1, KCONV):
            sums = sums + taps[k] * keep[k - 1] * pltpu.roll(ext, k, 1)[:, LANES:]
        before[rows, :] = raw[:, Q - LANES :]
        return silu(sums)

    def conv_all(ref, base):
        count = ref.shape[0]
        wide = ref[...].astype(F32)
        return jnp.concatenate([convolved(wide, at, base) for at in range(0, count, 8)], 0).astype(BF16)

    values = conv_all(value_ref, 0).astype(F32)
    input_map = conv_all(in_ref, inner)
    output_map = conv_all(out_ref, inner + LANES)
    map_ref[...] = output_map

    v = step_ref[...].astype(F32)[0:8, :] + vectors_ref[0, :, 0:1]
    step = jnp.maximum(v, 0.0) + jnp.log(1.0 + jnp.exp(-jnp.abs(v)))
    decay = vectors_ref[1, :, 0:1] * step
    jj = lax.broadcasted_iota(jnp.int32, (Q, Q), 0)
    ii = lax.broadcasted_iota(jnp.int32, (Q, Q), 1)
    causal = jj <= ii
    upper = jnp.where(causal, 1.0, 0.0).astype(BF16)
    running = sum(dot(part, upper) for part in thirds(decay))
    running_t = running.T
    barred = jnp.where(causal & (jj >= seg), 0.0, -1e30)
    last = running[:, Q - 1 : Q]
    last_seg = seg[:, Q - 1 : Q]
    carried = jnp.where(seg < 0, jnp.exp(running), 0.0)
    tail = jnp.where(place >= last_seg, jnp.exp(last - running), 0.0) * step
    reach_ref[...] = jnp.where(seg + first < 0, jnp.exp(total[:, 0:1] + running), 0.0)
    total[...] = total[...] + last
    scores = dot(input_map, output_map, ((0,), (0,)))
    entering = dot(state[...].astype(BF16), output_map)
    for head in range(heads):
        at = slice(head * head_width, (head + 1) * head_width)
        mine = values[at, :]
        factor = jnp.exp(running[head : head + 1, :] - running_t[:, head : head + 1] + barred)
        mixing = (scores * factor).astype(BF16)
        within = dot((mine * step[head : head + 1, :]).astype(BF16), mixing)
        skipped = jnp.concatenate([skip_ref[at, :]] * (Q // LANES), 1) * mine
        y_ref[at, :] = within + entering[at, :] * carried[head : head + 1, :] + skipped
        tailed = (mine * tail[head : head + 1, :]).astype(BF16)
        state[at, :] = carried[head : head + 1, Q - 1 : Q] * state[at, :] + dot(tailed, input_map, ((1,), (1,)))

    @pl.when(block == pl.num_programs(0) - 1)
    def _():
        state_ref[0:inner, :] = state[...]
        whole = jnp.where(last_seg + first < 0, jnp.exp(total[:, 0:1]), 0.0)
        state_ref[inner:, :] = jnp.broadcast_to(whole, (8, LANES))


def limits():
    return pltpu.CompilerParams(vmem_limit_bytes=48 * 1024 * 1024)


def whole(a):
    return pl.BlockSpec(a.shape, lambda i: (0,) * a.ndim)


def some(rows, columns, at=0):
    return pl.BlockSpec((rows, columns), lambda i: (at, i))


def ssd_pass(proj, rim, seg, taps, vectors, skip, heads, inner):
    count = proj.shape[1]
    maps = 2 * inner // LANES
    steps = 2 * inner + 2 * LANES
    return pl.pallas_call(
        functools.partial(ssd_kernel, heads),
        grid=(count // Q,),
        in_specs=[
            some(inner, Q),
            some(LANES, Q, maps),
            some(LANES, Q, maps + 1),
            some(16, Q, steps // 16),
            whole(rim),
            some(1, Q),
            whole(taps),
            whole(vectors),
            whole(skip),
        ],
        out_specs=[
            some(inner, Q),
            some(8, Q),
            some(LANES, Q),
            pl.BlockSpec((inner + 8, LANES), lambda i: (0, 0)),
        ],
        out_shape=[
            jax.ShapeDtypeStruct((inner, count), F32),
            jax.ShapeDtypeStruct((8, count), F32),
            jax.ShapeDtypeStruct((LANES, count), BF16),
            jax.ShapeDtypeStruct((inner + 8, LANES), F32),
        ],
        scratch_shapes=[
            pltpu.VMEM((inner + 2 * LANES, LANES), F32),
            pltpu.VMEM((inner, LANES), F32),
            pltpu.VMEM((8, LANES), F32),
        ],
        compiler_params=limits(),
        name="ssd_pass",
    )(proj, proj, proj, proj, rim, seg, taps, vectors, skip)


def gate_kernel(heads, *refs):
    parts = refs[:REACH]
    y_ref, reach_ref, map_ref, gate_ref, gated_ref, squares_ref, entering = refs[REACH:]
    inner = y_ref.shape[0]
    head_width = inner // heads

    @pl.when(pl.program_id(0) == 0)
    def _():
        for head in range(heads):
            at = slice(head * head_width, (head + 1) * head_width)
            sofar = parts[-1][at, :]
            for part in parts[-2::-1]:
                sofar = part[at, :] + part[inner + head : inner + head + 1, :] * sofar
            entering[at, :] = sofar.astype(BF16)

    carried = dot(entering[...], map_ref[...])
    squares = jnp.zeros((8, y_ref.shape[1]), F32)
    for head in range(heads):
        at = slice(head * head_width, (head + 1) * head_width)
        y = y_ref[at, :] + carried[at, :] * reach_ref[head : head + 1, :]
        gated = y * silu(gate_ref[at, :].astype(F32))
        gated_ref[at, :] = gated
        square = gated * gated
        squares = squares + sum(square[i : i + 8, :] for i in range(0, head_width, 8))
    squares_ref[...] = jnp.sum(squares, axis=0, keepdims=True)


def gate_pass(parts, y, reach, out_map, proj, heads):
    inner, count = y.shape
    step = 3 * Q
    return pl.pallas_call(
        functools.partial(gate_kernel, heads),
        grid=(count // step,),
        in_specs=[whole(p) for p in parts] + [some(inner, step), some(8, step), some(LANES, step), some(inner, step, 1)],
        out_specs=[some(inner, step), some(1, step)],
        out_shape=[
            jax.ShapeDtypeStruct((inner, count), F32),
            jax.ShapeDtypeStruct((1, count), F32),
        ],
        scratch_shapes=[pltpu.VMEM((inner, LANES), BF16)],
        compiler_params=limits(),
        name="gate_pass",
    )(*parts, y, reach, out_map, proj)


def norm_kernel(channels, parts, *refs):
    squares = refs[:parts]
    gated_ref, gain_ref, out_ref = refs[parts:]
    total = squares[0][...]
    for part in squares[1:]:
        total = total + part[...]
    scale = lax.rsqrt(total / channels + 1e-5)
    step = out_ref.shape[1]
    for at in range(0, out_ref.shape[0], 16):
        rows = slice(at, at + 16)
        gain = jnp.concatenate([gain_ref[rows, :]] * (step // LANES), 1)
        out_ref[rows, :] = (gated_ref[rows, :] * scale * gain).astype(BF16)


def norm_pass(squares, gated, gain, channels):
    inner, count = gated.shape
    step = 3 * Q
    return pl.pallas_call(
        functools.partial(norm_kernel, channels, len(squares)),
        grid=(count // step,),
        in_specs=[some(1, step) for _ in squares] + [some(inner, step), whole(gain)],
        out_specs=some(inner, step),
        out_shape=jax.ShapeDtypeStruct((inner, count), BF16),
        compiler_params=limits(),
        name="norm_pass",
    )(*squares, gated, gain)


def along_x(by):
    return [(z * SIDE + x, z * SIDE + (x + by) % SIDE) for z in range(SIDE) for x in range(SIDE)]


def along_z(by):
    return [(z * SIDE + x, (z + by) % SIDE * SIDE + x) for z in range(SIDE) for x in range(SIDE)]


def from_behind(array, by):
    length = lax.axis_size("seq")
    return lax.ppermute(array, "seq", [(i, i + by) for i in range(length - by)])


def on_device(
    hidden_rows,
    value_weight,
    gating_weight,
    state_weight,
    step_weight,
    value_kernel,
    state_kernel,
    step_bias,
    decay_log,
    skip_scale,
    norm_scale,
    document_lengths,
):
    members = lax.axis_size("tensor")
    count = hidden_rows.shape[0] * members
    inner = value_weight.shape[1]
    heads = step_weight.shape[1]
    head_width = inner // heads
    lanes = lambda a: jnp.broadcast_to(a[..., None], a.shape + (LANES,))
    joined = jnp.concatenate(
        [
            value_weight.T,
            gating_weight.T,
            state_weight.T,
            jnp.pad(step_weight.T, ((0, 16 - heads), (0, 0))),
        ],
        0,
    )
    taps = lanes(jnp.concatenate([value_kernel, state_kernel], 1))
    vectors = lanes(jnp.pad(jnp.stack([step_bias, -jnp.exp(decay_log)]), ((0, 0), (0, 8 - heads))))
    skip = lanes(jnp.repeat(skip_scale, head_width))
    gain = lanes(norm_scale)
    starts = jnp.cumsum(document_lengths) - document_lengths
    row_offset = lax.axis_index("seq") * count
    positions = row_offset + jnp.arange(count, dtype=jnp.int32)
    seg = jnp.max(jnp.where(positions[None, :] >= starts[:, None], starts[:, None], 0), axis=0) - row_offset
    seg = seg[None, :].astype(jnp.int32)

    gathered = lax.all_gather(hidden_rows, "tensor", axis=0, tiled=True)
    proj = dot(joined, gathered, ((1,), (1,))).astype(BF16)
    ends = proj[:, count - LANES :]
    rim = from_behind(jnp.concatenate([ends[:inner], ends[2 * inner : 2 * inner + 2 * LANES]], 0), 1)
    y, reach, out_map, summary = ssd_pass(proj, rim, seg, taps, vectors, skip, heads, inner)
    parts = [from_behind(summary, by) for by in range(1, REACH + 1)]
    gated, squares = gate_pass(parts, y, reach, out_map, proj, heads)
    row_sum = squares + sum(lax.ppermute(squares, "tensor", along_x(by)) for by in range(1, SIDE))
    shares = [row_sum] + [lax.ppermute(row_sum, "tensor", along_z(by)) for by in range(1, SIDE)]
    return norm_pass(shares, gated, gain, inner * members).T


def solution(mesh):
    in_specs = (
        P(("seq", "tensor"), None),
        P(None, "tensor"),
        P(None, "tensor"),
        P(),
        P(None, "tensor"),
        P(None, "tensor"),
        P(),
        P("tensor"),
        P("tensor"),
        P("tensor"),
        P("tensor"),
        P(),
    )
    out_specs = P("seq", "tensor")
    return jax.shard_map(
        on_device, mesh=mesh, in_specs=in_specs, out_specs=out_specs, check_vma=False
    )
```

```python
import functools

import jax
import jax.numpy as jnp
from jax import lax
from jax.experimental import pallas as pl
from jax.experimental.pallas import tpu as pltpu
from jax.sharding import PartitionSpec as P

KCONV = 4
Q = 256
LANES = 128
SIDE = 4
LIMIT = 24 * 1024 * 1024
REACH = 4
F32 = jnp.float32
BF16 = jnp.bfloat16


def dot(a, b, contract=((1,), (0,))):
    return lax.dot_general(a, b, (contract, ((), ())), preferred_element_type=F32)


def thirds(a):
    high = a.astype(BF16)
    rest = a - high.astype(F32)
    middle = rest.astype(BF16)
    return high, middle, (rest - middle.astype(F32)).astype(BF16)


def silu(v):
    half = 0.5 * v
    return half + half * jnp.tanh(half)


def block_kernel(heads, by, moves, arrays, kept, where_ref, *refs):
    weight_ref = refs[0]
    pieces = refs[1 : 1 + arrays]
    seg_ref, taps_ref, vectors_ref, skip_ref = refs[1 + arrays : 5 + arrays]
    y_ref, reach_ref, map_ref, gate_ref, state_ref = refs[5 + arrays + kept : 10 + arrays + kept]
    rows, projected, before, state, total, sems = refs[10 + arrays + kept :]
    inner = y_ref.shape[0]
    count = y_ref.shape[1]
    head_width = inner // heads
    maps = inner
    steps = maps + 2 * LANES
    gates = steps + 16
    copies = []
    for number, (array, source, place, offset, size) in enumerate(moves):
        target = LANES - 16
        if place >= 0:
            slot = (where_ref[1] + (0, 3, 1, 2)[place]) % SIDE
            target = pl.multiple_of(LANES + slot * (count // SIDE) + offset, 16)
        copies.append(
            pltpu.make_async_copy(
                pieces[array].at[pl.ds(source, size)], rows.at[pl.ds(target, size)], sems.at[number]
            )
        )
    for copy in copies:
        copy.start()
    state[...] = jnp.zeros_like(state)
    total[...] = jnp.zeros_like(total)
    jj = lax.broadcasted_iota(jnp.int32, (Q, Q), 0)
    ii = lax.broadcasted_iota(jnp.int32, (Q, Q), 1)
    causal = jj <= ii
    upper = jnp.where(causal, 1.0, 0.0).astype(BF16)
    place = lax.broadcasted_iota(jnp.int32, (1, Q), 1)
    origin = (where_ref[0] + by + SIDE) % SIDE * count
    for copy in copies:
        copy.wait()
    conv_rows = inner + 2 * LANES
    before[...] = dot(weight_ref[0:conv_rows, :], rows[0:LANES, :], ((1,), (1,))).astype(BF16).astype(F32)

    def project(chunk):
        projected[chunk % 2] = dot(weight_ref[...], rows[LANES + chunk * Q : LANES + (chunk + 1) * Q, :], ((1,), (1,))).astype(BF16)

    def recur(chunk):
        raw_ref = projected.at[chunk % 2]
        columns = slice(chunk * Q, (chunk + 1) * Q)
        gate_ref[:, columns] = raw_ref[gates : gates + inner, :]
        seg = seg_ref[:, columns] - (origin + chunk * Q)
        keep = [jnp.broadcast_to(jnp.where(place - k >= seg, 1.0, 0.0), (8, Q)) for k in range(1, KCONV)]

        def convolved(raw, base):
            rows_at = slice(base, base + 8)
            ext = jnp.concatenate([before[rows_at, :], raw], 1)
            taps = [jnp.concatenate([taps_ref[k, rows_at, :]] * (Q // LANES), 1) for k in range(KCONV)]
            sums = taps[0] * raw
            for k in range(1, KCONV):
                sums = sums + taps[k] * keep[k - 1] * pltpu.roll(ext, k, 1)[:, LANES:]
            before[rows_at, :] = raw[:, Q - LANES :]
            return silu(sums)

        def conv_all(start, size, base):
            wide = raw_ref[start : start + size, :].astype(F32)
            return jnp.concatenate(
                [convolved(wide[at : at + 8, :], base + at) for at in range(0, size, 8)], 0
            ).astype(BF16)

        values = conv_all(0, inner, 0).astype(F32)
        input_map = conv_all(maps, LANES, inner)
        output_map = conv_all(maps + LANES, LANES, inner + LANES)
        map_ref[:, columns] = output_map
        v = raw_ref[steps : steps + 16, :].astype(F32)[0:8, :] + vectors_ref[0, :, 0:1]
        step = jnp.maximum(v, 0.0) + jnp.log(1.0 + jnp.exp(-jnp.abs(v)))
        decay = vectors_ref[1, :, 0:1] * step
        running = sum(dot(part, upper) for part in thirds(decay))
        running_t = running.T
        barred = jnp.where(causal & (jj >= seg), 0.0, -1e30)
        last = running[:, Q - 1 : Q]
        last_seg = seg[:, Q - 1 : Q]
        carried = jnp.where(seg < 0, jnp.exp(running), 0.0)
        tail = jnp.where(place >= last_seg, jnp.exp(last - running), 0.0) * step
        reach_ref[:, columns] = jnp.where(seg + chunk * Q < 0, jnp.exp(total[:, 0:1] + running), 0.0)
        total[...] = total[...] + last
        scores = dot(input_map, output_map, ((0,), (0,)))
        entering = dot(state[...].astype(BF16), output_map) if chunk else None
        for head in range(heads):
            at = slice(head * head_width, (head + 1) * head_width)
            mine = values[at, :]
            factor = jnp.exp(running[head : head + 1, :] - running_t[:, head : head + 1] + barred)
            mixing = (scores * factor).astype(BF16)
            y = dot((mine * step[head : head + 1, :]).astype(BF16), mixing)
            if chunk:
                y = y + entering[at, :] * carried[head : head + 1, :]
            y_ref[at, columns] = y + jnp.concatenate([skip_ref[at, :]] * (Q // LANES), 1) * mine
            tailed = (mine * tail[head : head + 1, :]).astype(BF16)
            added = dot(tailed, input_map, ((1,), (1,)))
            state[at, :] = carried[head : head + 1, Q - 1 : Q] * state[at, :] + added if chunk else added
        if (chunk + 1) * Q == count:
            state_ref[0, 0:inner, :] = state[...]
            whole_way = jnp.where(last_seg + chunk * Q < 0, jnp.exp(total[:, 0:1]), 0.0)
            state_ref[0, inner:, :] = jnp.broadcast_to(whole_way, (8, LANES))

    chunks = count // Q
    project(0)
    for chunk in range(chunks):
        if chunk + 1 < chunks:
            project(chunk + 1)
        recur(chunk)


def limits():
    return pltpu.CompilerParams(vmem_limit_bytes=LIMIT)


def whole(a):
    return pl.BlockSpec(a.shape, lambda i: (0,) * a.ndim)


def some(rows, columns, at=0):
    return pl.BlockSpec((rows, columns), lambda i: (at, i))


def block_pass(where, by, joined, pieces, moves, seg, taps, vectors, skip, earlier, heads, inner):
    count = seg.shape[1]
    size = count // SIDE
    anywhere = pl.BlockSpec(memory_space=pl.ANY)
    across = lambda r: pl.BlockSpec((r, size), lambda i, w: (0, (w[0] + by + SIDE) % SIDE))
    return pl.pallas_call(
        functools.partial(block_kernel, heads, by, moves, len(pieces), len(earlier)),
        grid_spec=pltpu.PrefetchScalarGridSpec(
            num_scalar_prefetch=1,
            grid=(1,),
            in_specs=[pl.BlockSpec(memory_space=pltpu.VMEM)] + [anywhere] * len(pieces)
            + [
                across(1),
                *[pl.BlockSpec(memory_space=pltpu.VMEM)] * 3,
            ]
            + [anywhere] * len(earlier),
            out_specs=[
                across(inner),
                across(8),
                across(LANES),
                across(inner),
                pl.BlockSpec((1, inner + 8, LANES), lambda i, w: ((w[0] + by + SIDE) % SIDE, 0, 0)),
            ],
            scratch_shapes=[
                pltpu.VMEM((LANES + size, joined.shape[1]), BF16),
                pltpu.VMEM((2, joined.shape[0], Q), BF16),
                pltpu.VMEM((inner + 2 * LANES, LANES), F32),
                pltpu.VMEM((inner, LANES), F32),
                pltpu.VMEM((8, LANES), F32),
                pltpu.SemaphoreType.DMA((len(moves),)),
            ],
        ),
        out_shape=[
            jax.ShapeDtypeStruct((inner, count), F32),
            jax.ShapeDtypeStruct((8, count), F32),
            jax.ShapeDtypeStruct((LANES, count), BF16),
            jax.ShapeDtypeStruct((inner, count), BF16),
            jax.ShapeDtypeStruct((SIDE, inner + 8, LANES), F32),
        ],
        input_output_aliases={6 + len(pieces) + i: i for i in range(len(earlier))},
        compiler_params=limits(),
        cost_estimate=pl.CostEstimate(
            flops=2 * size * joined.shape[0] * joined.shape[1] * 2, bytes_accessed=20 << 20, transcendentals=1 << 21
        ),
        name="block_pass",
    )(where, joined, *pieces, seg, taps, vectors, skip, *earlier)


def gate_kernel(heads, *refs):
    parts = refs[:REACH]
    state_ref, y_ref, reach_ref, map_ref, gate_ref, gated_ref, squares_ref, entering = refs[REACH:]
    inner = y_ref.shape[0]
    head_width = inner // heads
    block = pl.program_id(0)

    @pl.when(block == 0)
    def _():
        for head in range(heads):
            at = slice(head * head_width, (head + 1) * head_width)
            sofar = parts[-1][at, :].astype(F32)
            for part in parts[-2::-1]:
                sofar = part[at, :].astype(F32) + part[inner : inner + 16, :].astype(F32)[head : head + 1, :] * sofar
            entering[at, :] = sofar

    @pl.when(block > 0)
    def _():
        for head in range(heads):
            at = slice(head * head_width, (head + 1) * head_width)
            entering[at, :] = state_ref[0, at, :] + state_ref[0, inner + head : inner + head + 1, :] * entering[at, :]

    carried = dot(entering[...].astype(BF16), map_ref[...])
    squares = jnp.zeros((8, y_ref.shape[1]), F32)
    for head in range(heads):
        at = slice(head * head_width, (head + 1) * head_width)
        y = y_ref[at, :] + carried[at, :] * reach_ref[head : head + 1, :]
        gated = y * silu(gate_ref[at, :].astype(F32))
        gated_ref[at, :] = gated
        square = gated * gated
        squares = squares + sum(square[i : i + 8, :] for i in range(0, head_width, 8))
    squares_ref[...] = jnp.sum(squares, axis=0, keepdims=True)


def gate_pass(parts, states, y, reach, out_map, gating, heads):
    inner, count = y.shape
    step = count // SIDE
    return pl.pallas_call(
        functools.partial(gate_kernel, heads),
        grid=(SIDE,),
        in_specs=[whole(p) for p in parts]
        + [pl.BlockSpec((1,) + states.shape[1:], lambda i: (jnp.maximum(i - 1, 0), 0, 0))]
        + [some(inner, step), some(8, step), some(LANES, step), some(inner, step)],
        out_specs=[some(inner, step), some(1, step)],
        out_shape=[
            jax.ShapeDtypeStruct((inner, count), F32),
            jax.ShapeDtypeStruct((1, count), F32),
        ],
        scratch_shapes=[pltpu.VMEM((inner, LANES), F32)],
        compiler_params=limits(),
        name="gate_pass",
    )(*parts, states, y, reach, out_map, gating)


def norm_kernel(channels, squares_ref, gated_ref, gain_ref, out_ref):
    total = jnp.sum(squares_ref[...], axis=0, keepdims=True)
    scale = lax.rsqrt(total / channels + 1e-5)
    step = out_ref.shape[1]
    for at in range(0, out_ref.shape[0], 16):
        rows = slice(at, at + 16)
        gain = jnp.concatenate([gain_ref[rows, :]] * (step // LANES), 1)
        out_ref[rows, :] = (gated_ref[rows, :] * scale * gain).astype(BF16)


def norm_pass(squares, gated, gain, channels):
    inner, count = gated.shape
    step = 3 * Q
    return pl.pallas_call(
        functools.partial(norm_kernel, channels),
        grid=(count // step,),
        in_specs=[some(squares.shape[0], step), some(inner, step), whole(gain)],
        out_specs=some(inner, step),
        out_shape=jax.ShapeDtypeStruct((inner, count), BF16),
        compiler_params=limits(),
        name="norm_pass",
    )(squares, gated, gain)


def along_x(by):
    return [(z * SIDE + x, z * SIDE + (x + by) % SIDE) for z in range(SIDE) for x in range(SIDE)]


def along_z(by):
    return [(z * SIDE + x, (z + by) % SIDE * SIDE + x) for z in range(SIDE) for x in range(SIDE)]


def next_line(array, target):
    lines = lax.axis_size("seq") * SIDE
    pairs = [(i * SIDE + SIDE - 1, i * SIDE + SIDE + target) for i in range(lines - 1)]
    return lax.ppermute(array, ("seq", "tensor"), pairs)


def from_behind(array, by):
    length = lax.axis_size("seq")
    return lax.ppermute(array, "seq", [(i, i + by) for i in range(length - by)])


def on_device(
    hidden_rows,
    value_weight,
    gating_weight,
    state_weight,
    step_weight,
    value_kernel,
    state_kernel,
    step_bias,
    decay_log,
    skip_scale,
    norm_scale,
    document_lengths,
):
    members = lax.axis_size("tensor")
    count = hidden_rows.shape[0] * members
    inner = value_weight.shape[1]
    heads = step_weight.shape[1]
    head_width = inner // heads
    lanes = lambda a: jnp.broadcast_to(a[..., None], a.shape + (LANES,))
    joined = jnp.concatenate(
        [
            value_weight.T,
            state_weight.T,
            jnp.pad(step_weight.T, ((0, 16 - heads), (0, 0))),
            gating_weight.T,
        ],
        0,
    )
    taps = lanes(jnp.concatenate([value_kernel, state_kernel], 1))
    vectors = lanes(jnp.pad(jnp.stack([step_bias, -jnp.exp(decay_log)]), ((0, 0), (0, 8 - heads))))
    skip = lanes(jnp.repeat(skip_scale, head_width))
    gain = lanes(norm_scale)
    starts = jnp.cumsum(document_lengths) - document_lengths
    row_offset = lax.axis_index("seq") * count
    positions = row_offset + jnp.arange(count, dtype=jnp.int32)
    seg = jnp.max(jnp.where(positions[None, :] >= starts[:, None], starts[:, None], 0), axis=0) - row_offset
    seg = seg[None, :].astype(jnp.int32)

    own = hidden_rows
    size = own.shape[0]
    half = size // 2
    part_a, part_b = size * 5 // 12, size * 7 // 12
    cut = part_b * 4 // 7
    x_step = lambda a, by: lax.ppermute(a, "tensor", along_x(by))
    z_step = lambda a, by: lax.ppermute(a, "tensor", along_z(by))
    place = lax.axis_index("tensor")
    z, x = place // SIDE, place % SIDE

    x_back, x_ahead = x_step(own, 1), x_step(own, -1)
    z_back, z_ahead = z_step(own[part_a:], 1), z_step(own[part_a:], -1)
    tail = own[size - 16 :]
    rim_1, rim_3 = next_line(tail, 1), next_line(tail, 3)
    x_far_1 = x_step(jnp.concatenate([x_back[:half], rim_3], 0), 1)
    x_far_2 = x_step(jnp.concatenate([x_ahead[half:], rim_3], 0), -1)
    z_far_1, z_far_2 = z_step(z_back[:cut], 1), z_step(z_ahead[cut:], -1)
    first = jnp.concatenate([own[:part_a], x_back[:part_a], x_ahead[:part_a]], 0)
    first_back, first_ahead = z_step(first, 1), z_step(first, -1)
    x_far_1, x_far_2, z_back, z_ahead = lax.optimization_barrier((x_far_1, x_far_2, z_back, z_ahead))
    near = jnp.concatenate([z_back, z_ahead], 0)
    near_1, near_2 = x_step(near, 1), x_step(near, -1)
    rim = lax.select_n(x, x_far_1[half:], rim_1, x_far_2[half:], rim_3)
    where = jnp.stack([z, x]).astype(jnp.int32)

    def run(by, pieces, moves, earlier):
        return block_pass(where, by, joined, pieces, moves, seg, taps, vectors, skip, earlier, heads, inner)

    done = run(
        0,
        [own, x_back, x_ahead, x_far_1, x_far_2, rim],
        (
            (0, 0, 0, 0, size),
            (1, 0, 1, 0, size),
            (2, 0, 2, 0, size),
            (3, 0, 3, 0, half),
            (4, 0, 3, half, half),
            (5, 0, -1, 0, 16),
        ),
        [],
    )
    rim, done = lax.optimization_barrier((rim, done))
    second = jnp.concatenate([x_far_1[:part_a], rim], 0)
    second_back, second_ahead = z_step(second, 1), z_step(second, -1)
    near_far_1, near_far_2 = x_step(near_1[:part_b], 1), x_step(near_2[part_b:], -1)
    z_far_1, near_far_1, near_far_2 = lax.optimization_barrier((z_far_1, near_far_1, near_far_2))
    far = jnp.concatenate([z_far_1, z_far_2], 0)
    far_1, far_2 = x_step(far, 1), x_step(far, -1)
    last = jnp.concatenate([first_ahead[2 * part_a :], second_ahead], 0)
    line_far_1, line_far_2 = z_step(first_back[: 2 * part_a], 1), z_step(last, -1)
    far_far_1, far_far_2 = x_step(far_1[:cut], 1), x_step(far_2[cut:], -1)
    lines = tuple((0, part_a * i, i, 0, part_a) for i in range(3)) + ((1, 0, 3, 0, part_a), (1, part_a, -1, 0, 16))
    done = run(
        -1,
        [first_back, second_back, z_back, near_1, near_2, near_far_1],
        lines + tuple((2 + i, 0, i, part_a, part_b) for i in range(SIDE)),
        done,
    )
    done = run(
        1,
        [first_ahead, second_ahead, z_ahead, near_1, near_2, near_far_2],
        lines
        + (
            (2, 0, 0, part_a, part_b),
            (3, part_b, 1, part_a, part_b),
            (4, part_b, 2, part_a, part_b),
            (5, 0, 3, part_a, part_b),
        ),
        done,
    )
    y, reach, out_map, gating, states = run(
        2,
        [line_far_1, line_far_2, far, far_1, far_2, far_far_1, far_far_2],
        (
            (0, 0, 0, 0, part_a),
            (0, part_a, 1, 0, part_a),
            (1, 0, 2, 0, part_a),
            (1, part_a, 3, 0, part_a),
            (1, 2 * part_a, -1, 0, 16),
            (2, 0, 0, part_a, part_b),
            (3, 0, 1, part_a, part_b),
            (4, 0, 2, part_a, part_b),
            (5, 0, 3, part_a, cut),
            (6, 0, 3, part_a + cut, part_b - cut),
        ),
        done,
    )
    through, summary = states[0, inner:], states[0, :inner]
    for later in states[1:]:
        across = jnp.repeat(later[inner : inner + heads], head_width, axis=0)
        through, summary = through * later[inner:], later[:inner] + across * summary
    summary = jnp.concatenate([summary, through, jnp.zeros_like(through)], 0).astype(BF16)
    parts = [from_behind(summary, by) for by in range(1, REACH + 1)]
    gated, squares = gate_pass(parts, states, y, reach, out_map, gating, heads)
    shares = lax.all_to_all(jnp.broadcast_to(squares, (members, count)), "tensor", 0, 0, tiled=True)
    return norm_pass(shares, gated, gain, inner * members).T


def solution(mesh):
    in_specs = (
        P(("seq", "tensor"), None),
        P(None, "tensor"),
        P(None, "tensor"),
        P(),
        P(None, "tensor"),
        P(None, "tensor"),
        P(),
        P("tensor"),
        P("tensor"),
        P("tensor"),
        P("tensor"),
        P(),
    )
    out_specs = P("seq", "tensor")
    return jax.shard_map(
        on_device, mesh=mesh, in_specs=in_specs, out_specs=out_specs, check_vma=False
    )
```

```python
import functools

import jax
import jax.numpy as jnp
from jax import lax
from jax.experimental import pallas as pl
from jax.experimental.pallas import tpu as pltpu
from jax.sharding import PartitionSpec as P

KCONV = 4
Q = 256
LANES = 128
SIDE = 4
LIMIT = 24 * 1024 * 1024
REACH = 4
F32 = jnp.float32
BF16 = jnp.bfloat16


def dot(a, b, contract=((1,), (0,))):
    return lax.dot_general(a, b, (contract, ((), ())), preferred_element_type=F32)


def thirds(a):
    high = a.astype(BF16)
    rest = a - high.astype(F32)
    middle = rest.astype(BF16)
    return high, middle, (rest - middle.astype(F32)).astype(BF16)


def silu(v):
    half = 0.5 * v
    return half + half * jnp.tanh(half)


def block_kernel(heads, by, moves, arrays, kept, where_ref, *refs):
    weight_ref = refs[0]
    pieces = refs[1 : 1 + arrays]
    seg_ref, taps_ref, vectors_ref, skip_ref = refs[1 + arrays : 5 + arrays]
    y_ref, reach_ref, map_ref, gate_ref, state_ref = refs[5 + arrays + kept : 10 + arrays + kept]
    rows, projected, before, state, total, sems = refs[10 + arrays + kept :]
    inner = y_ref.shape[0]
    count = y_ref.shape[1]
    head_width = inner // heads
    maps = inner
    steps = maps + 2 * LANES
    gates = steps + 16
    copies = []
    for number, (array, source, place, offset, size) in enumerate(moves):
        target = LANES - 16
        if place >= 0:
            slot = (where_ref[1] + (0, 3, 1, 2)[place]) % SIDE
            target = pl.multiple_of(LANES + slot * (count // SIDE) + offset, 16)
        copies.append(
            pltpu.make_async_copy(
                pieces[array].at[pl.ds(source, size)], rows.at[pl.ds(target, size)], sems.at[number]
            )
        )
    for copy in copies:
        copy.start()
    state[...] = jnp.zeros_like(state)
    total[...] = jnp.zeros_like(total)
    jj = lax.broadcasted_iota(jnp.int32, (Q, Q), 0)
    ii = lax.broadcasted_iota(jnp.int32, (Q, Q), 1)
    causal = jj <= ii
    upper = jnp.where(causal, 1.0, 0.0).astype(BF16)
    place = lax.broadcasted_iota(jnp.int32, (1, Q), 1)
    origin = (where_ref[0] + by + SIDE) % SIDE * count
    for copy in copies:
        copy.wait()
    conv_rows = inner + 2 * LANES
    before[...] = dot(weight_ref[0:conv_rows, :], rows[0:LANES, :], ((1,), (1,))).astype(BF16).astype(F32)

    def project(chunk, part=None):
        ends = (0, inner, gates, gates + inner)
        at = slice(0, gates + inner) if part is None else slice(ends[part], ends[part + 1])
        now = rows[LANES + chunk * Q : LANES + (chunk + 1) * Q, :]
        projected[chunk % 2, at, :] = dot(weight_ref[at, :], now, ((1,), (1,))).astype(BF16)

    def recur(chunk):
        ahead = (lambda part: project(chunk + 1, part)) if (chunk + 1) * Q < count else (lambda part: None)
        raw_ref = projected.at[chunk % 2]
        columns = slice(chunk * Q, (chunk + 1) * Q)
        gate_ref[:, columns] = raw_ref[gates : gates + inner, :]
        seg = seg_ref[:, columns] - (origin + chunk * Q)
        keep = [jnp.broadcast_to(jnp.where(place - k >= seg, 1.0, 0.0), (8, Q)) for k in range(1, KCONV)]

        def convolved(raw, base):
            rows_at = slice(base, base + 8)
            ext = jnp.concatenate([before[rows_at, :], raw], 1)
            taps = [jnp.concatenate([taps_ref[k, rows_at, :]] * (Q // LANES), 1) for k in range(KCONV)]
            sums = taps[0] * raw
            for k in range(1, KCONV):
                sums = sums + taps[k] * keep[k - 1] * pltpu.roll(ext, k, 1)[:, LANES:]
            before[rows_at, :] = raw[:, Q - LANES :]
            return silu(sums)

        def conv_all(start, size, base):
            wide = raw_ref[start : start + size, :].astype(F32)
            return jnp.concatenate(
                [convolved(wide[at : at + 8, :], base + at) for at in range(0, size, 8)], 0
            ).astype(BF16)

        ahead(0)
        values = conv_all(0, inner, 0).astype(F32)
        ahead(1)
        input_map = conv_all(maps, LANES, inner)
        output_map = conv_all(maps + LANES, LANES, inner + LANES)
        map_ref[:, columns] = output_map
        v = raw_ref[steps : steps + 16, :].astype(F32)[0:8, :] + vectors_ref[0, :, 0:1]
        step = jnp.maximum(v, 0.0) + jnp.log(1.0 + jnp.exp(-jnp.abs(v)))
        decay = vectors_ref[1, :, 0:1] * step
        running = sum(dot(part, upper) for part in thirds(decay))
        running_t = running.T
        barred = jnp.where(causal & (jj >= seg), 0.0, -1e30)
        last = running[:, Q - 1 : Q]
        last_seg = seg[:, Q - 1 : Q]
        carried = jnp.where(seg < 0, jnp.exp(running), 0.0)
        tail = jnp.where(place >= last_seg, jnp.exp(last - running), 0.0) * step
        reach_ref[:, columns] = jnp.where(seg + chunk * Q < 0, jnp.exp(total[:, 0:1] + running), 0.0)
        total[...] = total[...] + last
        scores = dot(input_map, output_map, ((0,), (0,)))
        entering = dot(state[...].astype(BF16), output_map) if chunk else None
        ahead(2)
        for head in range(heads):
            at = slice(head * head_width, (head + 1) * head_width)
            mine = values[at, :]
            factor = jnp.exp(running[head : head + 1, :] - running_t[:, head : head + 1] + barred)
            mixing = (scores * factor).astype(BF16)
            y = dot((mine * step[head : head + 1, :]).astype(BF16), mixing)
            if chunk:
                y = y + entering[at, :] * carried[head : head + 1, :]
            y_ref[at, columns] = y + jnp.concatenate([skip_ref[at, :]] * (Q // LANES), 1) * mine
            tailed = (mine * tail[head : head + 1, :]).astype(BF16)
            added = dot(tailed, input_map, ((1,), (1,)))
            state[at, :] = carried[head : head + 1, Q - 1 : Q] * state[at, :] + added if chunk else added
        if (chunk + 1) * Q == count:
            state_ref[0, 0:inner, :] = state[...]
            whole_way = jnp.where(last_seg + chunk * Q < 0, jnp.exp(total[:, 0:1]), 0.0)
            state_ref[0, inner:, :] = jnp.broadcast_to(whole_way, (8, LANES))

    chunks = count // Q
    project(0)
    for chunk in range(chunks):
        recur(chunk)


def limits():
    return pltpu.CompilerParams(vmem_limit_bytes=LIMIT)


def whole(a):
    return pl.BlockSpec(a.shape, lambda i: (0,) * a.ndim)


def some(rows, columns, at=0):
    return pl.BlockSpec((rows, columns), lambda i: (at, i))


def block_pass(where, by, joined, pieces, moves, seg, taps, vectors, skip, earlier, heads, inner):
    count = seg.shape[1]
    size = count // SIDE
    anywhere = pl.BlockSpec(memory_space=pl.ANY)
    across = lambda r: pl.BlockSpec((r, size), lambda i, w: (0, (w[0] + by + SIDE) % SIDE))
    return pl.pallas_call(
        functools.partial(block_kernel, heads, by, moves, len(pieces), len(earlier)),
        grid_spec=pltpu.PrefetchScalarGridSpec(
            num_scalar_prefetch=1,
            grid=(1,),
            in_specs=[pl.BlockSpec(memory_space=pltpu.VMEM)] + [anywhere] * len(pieces)
            + [
                across(1),
                *[pl.BlockSpec(memory_space=pltpu.VMEM)] * 3,
            ]
            + [anywhere] * len(earlier),
            out_specs=[
                across(inner),
                across(8),
                across(LANES),
                across(inner),
                pl.BlockSpec((1, inner + 8, LANES), lambda i, w: ((w[0] + by + SIDE) % SIDE, 0, 0)),
            ],
            scratch_shapes=[
                pltpu.VMEM((LANES + size, joined.shape[1]), BF16),
                pltpu.VMEM((2, joined.shape[0], Q), BF16),
                pltpu.VMEM((inner + 2 * LANES, LANES), F32),
                pltpu.VMEM((inner, LANES), F32),
                pltpu.VMEM((8, LANES), F32),
                pltpu.SemaphoreType.DMA((len(moves),)),
            ],
        ),
        out_shape=[
            jax.ShapeDtypeStruct((inner, count), F32),
            jax.ShapeDtypeStruct((8, count), F32),
            jax.ShapeDtypeStruct((LANES, count), BF16),
            jax.ShapeDtypeStruct((inner, count), BF16),
            jax.ShapeDtypeStruct((SIDE, inner + 8, LANES), F32),
        ],
        input_output_aliases={6 + len(pieces) + i: i for i in range(len(earlier))},
        compiler_params=limits(),
        cost_estimate=pl.CostEstimate(
            flops=2 * size * joined.shape[0] * joined.shape[1] * 2, bytes_accessed=20 << 20, transcendentals=1 << 21
        ),
        name="block_pass",
    )(where, joined, *pieces, seg, taps, vectors, skip, *earlier)


def gate_kernel(heads, *refs):
    parts = refs[:REACH]
    state_ref, y_ref, reach_ref, map_ref, gate_ref, gated_ref, squares_ref, entering = refs[REACH:]
    inner = y_ref.shape[0]
    head_width = inner // heads
    block = pl.program_id(0)

    @pl.when(block == 0)
    def _():
        for head in range(heads):
            at = slice(head * head_width, (head + 1) * head_width)
            sofar = parts[-1][at, :].astype(F32)
            for part in parts[-2::-1]:
                sofar = part[at, :].astype(F32) + part[inner : inner + 16, :].astype(F32)[head : head + 1, :] * sofar
            entering[at, :] = sofar

    @pl.when(block > 0)
    def _():
        for head in range(heads):
            at = slice(head * head_width, (head + 1) * head_width)
            entering[at, :] = state_ref[0, at, :] + state_ref[0, inner + head : inner + head + 1, :] * entering[at, :]

    carried = dot(entering[...].astype(BF16), map_ref[...])
    squares = jnp.zeros((8, y_ref.shape[1]), F32)
    for head in range(heads):
        at = slice(head * head_width, (head + 1) * head_width)
        y = y_ref[at, :] + carried[at, :] * reach_ref[head : head + 1, :]
        gated = y * silu(gate_ref[at, :].astype(F32))
        gated_ref[at, :] = gated
        square = gated * gated
        squares = squares + sum(square[i : i + 8, :] for i in range(0, head_width, 8))
    squares_ref[...] = jnp.sum(squares, axis=0, keepdims=True)


def gate_pass(parts, states, y, reach, out_map, gating, heads):
    inner, count = y.shape
    step = count // SIDE
    return pl.pallas_call(
        functools.partial(gate_kernel, heads),
        grid=(SIDE,),
        in_specs=[whole(p) for p in parts]
        + [pl.BlockSpec((1,) + states.shape[1:], lambda i: (jnp.maximum(i - 1, 0), 0, 0))]
        + [some(inner, step), some(8, step), some(LANES, step), some(inner, step)],
        out_specs=[some(inner, step), some(1, step)],
        out_shape=[
            jax.ShapeDtypeStruct((inner, count), F32),
            jax.ShapeDtypeStruct((1, count), F32),
        ],
        scratch_shapes=[pltpu.VMEM((inner, LANES), F32)],
        compiler_params=limits(),
        name="gate_pass",
    )(*parts, states, y, reach, out_map, gating)


def norm_kernel(channels, squares_ref, gated_ref, gain_ref, out_ref):
    total = jnp.sum(squares_ref[...], axis=0, keepdims=True)
    scale = lax.rsqrt(total / channels + 1e-5)
    step = out_ref.shape[1]
    for at in range(0, out_ref.shape[0], 16):
        rows = slice(at, at + 16)
        gain = jnp.concatenate([gain_ref[rows, :]] * (step // LANES), 1)
        out_ref[rows, :] = (gated_ref[rows, :] * scale * gain).astype(BF16)


def norm_pass(squares, gated, gain, channels):
    inner, count = gated.shape
    step = 3 * Q
    return pl.pallas_call(
        functools.partial(norm_kernel, channels),
        grid=(count // step,),
        in_specs=[some(squares.shape[0], step), some(inner, step), whole(gain)],
        out_specs=some(inner, step),
        out_shape=jax.ShapeDtypeStruct((inner, count), BF16),
        compiler_params=limits(),
        name="norm_pass",
    )(squares, gated, gain)


def along_x(by):
    return [(z * SIDE + x, z * SIDE + (x + by) % SIDE) for z in range(SIDE) for x in range(SIDE)]


def along_z(by):
    return [(z * SIDE + x, (z + by) % SIDE * SIDE + x) for z in range(SIDE) for x in range(SIDE)]


def next_line(array, target):
    lines = lax.axis_size("seq") * SIDE
    pairs = [(i * SIDE + SIDE - 1, i * SIDE + SIDE + target) for i in range(lines - 1)]
    return lax.ppermute(array, ("seq", "tensor"), pairs)


def from_behind(array, by):
    length = lax.axis_size("seq")
    return lax.ppermute(array, "seq", [(i, i + by) for i in range(length - by)])


def on_device(
    hidden_rows,
    value_weight,
    gating_weight,
    state_weight,
    step_weight,
    value_kernel,
    state_kernel,
    step_bias,
    decay_log,
    skip_scale,
    norm_scale,
    document_lengths,
):
    members = lax.axis_size("tensor")
    count = hidden_rows.shape[0] * members
    inner = value_weight.shape[1]
    heads = step_weight.shape[1]
    head_width = inner // heads
    lanes = lambda a: jnp.broadcast_to(a[..., None], a.shape + (LANES,))
    joined = jnp.concatenate(
        [
            value_weight.T,
            state_weight.T,
            jnp.pad(step_weight.T, ((0, 16 - heads), (0, 0))),
            gating_weight.T,
        ],
        0,
    )
    taps = lanes(jnp.concatenate([value_kernel, state_kernel], 1))
    vectors = lanes(jnp.pad(jnp.stack([step_bias, -jnp.exp(decay_log)]), ((0, 0), (0, 8 - heads))))
    skip = lanes(jnp.repeat(skip_scale, head_width))
    gain = lanes(norm_scale)
    starts = jnp.cumsum(document_lengths) - document_lengths
    row_offset = lax.axis_index("seq") * count
    positions = row_offset + jnp.arange(count, dtype=jnp.int32)
    seg = jnp.max(jnp.where(positions[None, :] >= starts[:, None], starts[:, None], 0), axis=0) - row_offset
    seg = seg[None, :].astype(jnp.int32)

    own = hidden_rows
    size = own.shape[0]
    half = size // 2
    part_a, part_b = size * 5 // 12, size * 7 // 12
    cut = part_b * 4 // 7
    x_step = lambda a, by: lax.ppermute(a, "tensor", along_x(by))
    z_step = lambda a, by: lax.ppermute(a, "tensor", along_z(by))
    place = lax.axis_index("tensor")
    z, x = place // SIDE, place % SIDE

    x_back, x_ahead = x_step(own, 1), x_step(own, -1)
    z_back, z_ahead = z_step(own[part_a:], 1), z_step(own[part_a:], -1)
    tail = own[size - 16 :]
    rim_1, rim_3 = next_line(tail, 1), next_line(tail, 3)
    x_far_1 = x_step(jnp.concatenate([x_back[:half], rim_3], 0), 1)
    x_far_2 = x_step(jnp.concatenate([x_ahead[half:], rim_3], 0), -1)
    z_far_1, z_far_2 = z_step(z_back[:cut], 1), z_step(z_ahead[cut:], -1)
    first = jnp.concatenate([own[:part_a], x_back[:part_a], x_ahead[:part_a]], 0)
    first_back, first_ahead = z_step(first, 1), z_step(first, -1)
    x_far_1, x_far_2, z_back, z_ahead = lax.optimization_barrier((x_far_1, x_far_2, z_back, z_ahead))
    near = jnp.concatenate([z_back, z_ahead], 0)
    near_1, near_2 = x_step(near, 1), x_step(near, -1)
    rim = lax.select_n(x, x_far_1[half:], rim_1, x_far_2[half:], rim_3)
    where = jnp.stack([z, x]).astype(jnp.int32)

    def run(by, pieces, moves, earlier):
        return block_pass(where, by, joined, pieces, moves, seg, taps, vectors, skip, earlier, heads, inner)

    done = run(
        0,
        [own, x_back, x_ahead, x_far_1, x_far_2, rim],
        (
            (0, 0, 0, 0, size),
            (1, 0, 1, 0, size),
            (2, 0, 2, 0, size),
            (3, 0, 3, 0, half),
            (4, 0, 3, half, half),
            (5, 0, -1, 0, 16),
        ),
        [],
    )
    rim, done = lax.optimization_barrier((rim, done))
    second = jnp.concatenate([x_far_1[:part_a], rim], 0)
    second_back, second_ahead = z_step(second, 1), z_step(second, -1)
    near_far_1, near_far_2 = x_step(near_1[:part_b], 1), x_step(near_2[part_b:], -1)
    z_far_1, near_far_1, near_far_2 = lax.optimization_barrier((z_far_1, near_far_1, near_far_2))
    far = jnp.concatenate([z_far_1, z_far_2], 0)
    far_1, far_2, far_3 = x_step(far, 1), x_step(far, -1), x_step(far, 2)
    last = jnp.concatenate([first_ahead[2 * part_a :], second_ahead], 0)
    line_far_1, line_far_2 = z_step(first_back[: 2 * part_a], 1), z_step(last, -1)
    lines = tuple((0, part_a * i, i, 0, part_a) for i in range(3)) + ((1, 0, 3, 0, part_a), (1, part_a, -1, 0, 16))
    done = run(
        -1,
        [first_back, second_back, z_back, near_1, near_2, near_far_1],
        lines + tuple((2 + i, 0, i, part_a, part_b) for i in range(SIDE)),
        done,
    )
    done = run(
        1,
        [first_ahead, second_ahead, z_ahead, near_1, near_2, near_far_2],
        lines
        + (
            (2, 0, 0, part_a, part_b),
            (3, part_b, 1, part_a, part_b),
            (4, part_b, 2, part_a, part_b),
            (5, 0, 3, part_a, part_b),
        ),
        done,
    )
    y, reach, out_map, gating, states = run(
        2,
        [line_far_1, line_far_2, far, far_1, far_2, far_3],
        (
            (0, 0, 0, 0, part_a),
            (0, part_a, 1, 0, part_a),
            (1, 0, 2, 0, part_a),
            (1, part_a, 3, 0, part_a),
            (1, 2 * part_a, -1, 0, 16),
        )
        + tuple((2 + i, 0, i, part_a, part_b) for i in range(SIDE)),
        done,
    )
    through, summary = states[0, inner:], states[0, :inner]
    for later in states[1:]:
        across = jnp.repeat(later[inner : inner + heads], head_width, axis=0)
        through, summary = through * later[inner:], later[:inner] + across * summary
    summary = jnp.concatenate([summary, through, jnp.zeros_like(through)], 0).astype(BF16)
    parts = [from_behind(summary, by) for by in range(1, REACH + 1)]
    gated, squares = gate_pass(parts, states, y, reach, out_map, gating, heads)
    shares = lax.all_to_all(jnp.broadcast_to(squares, (members, count)), "tensor", 0, 0, tiled=True)
    return norm_pass(shares, gated, gain, inner * members).T


def solution(mesh):
    in_specs = (
        P(("seq", "tensor"), None),
        P(None, "tensor"),
        P(None, "tensor"),
        P(),
        P(None, "tensor"),
        P(None, "tensor"),
        P(),
        P("tensor"),
        P("tensor"),
        P("tensor"),
        P("tensor"),
        P(),
    )
    out_specs = P("seq", "tensor")
    return jax.shard_map(
        on_device, mesh=mesh, in_specs=in_specs, out_specs=out_specs, check_vma=False
    )
```
